256 devices in a mesh: dp: 16 (over y_lo, x, core), task: 16 (over z, y_hi).
Axes of the slice: x: 4, y: 4 (y_hi: 2, y_lo: 2; y = y_hi * 2 + y_lo), z: 8, core: 2. Of those that a mesh axis runs over, the one named last changes fastest.
Arguments:
- features: bfloat16 [4096, 8, 512], P(('dp', 'task')), may hold values from -6 to 6
- task_embed: bfloat16 [8192, 512], P('task'), may hold values from -0.25 to 0.25
- bin_bias: float32 [8192, 8], P('task'), may hold values from -2 to 0.5
- bin_bounds: int32 [9], replicated, may hold values from 0 to 640, as said below
- event_time: int32 [4096, 8192], P('dp', 'task'), may hold values from 1 to 639
- censored: int32 [4096, 8192], P('dp', 'task'), may hold values 0 or 1
- at_risk: int32 [32, 64], P('dp', 'task'), may hold values from 0 to 1
Outputs:
- grad_features: bfloat16 [4096, 8, 512], P(('dp', 'task'))
- grad_embed: float32 [8192, 512], P(('task', 'dp'))
- grad_bias: float32 [8192, 8], P(('task', 'dp'))
The draws below stay inside these ranges and needn't reach their ends.
Inputs may be any that keep to these rules, and one draw needn't show every extreme that they name: bin_bounds[0] is 0, bin_bounds[8] is 640, and the bounds rise strictly.
All inputs are finite; a program needn't handle non-finite values. No bound on the sum of `censored` on one device may be relied on, other than what follows from the above.
Results may differ from the reference program's by a relative error of at most 0.0045.
Values may be sent and summed in bfloat16 or wider, within the bound.
No kernel may reach another device: no remote copies, remote signals or barrier semaphores. Data moves between devices by JAX's collectives and lax.ppermute only.
A program may use at most 64 MiB of HBM per device.

```python
import jax
import jax.numpy as jnp
from jax import lax

E = 512
BINS = 8
TASKS = 8192
TB = 128
TOKENS = 4096


def draw_bin_bounds(key, part):
    key = jax.random.fold_in(key, 11)
    steps_drawn = jax.random.randint(key, (BINS - 1,), 16, 80)
    inner = jnp.cumsum(steps_drawn).astype(jnp.int32)
    return jnp.concatenate([jnp.zeros((1,), jnp.int32), inner, jnp.full((1,), 640, jnp.int32)])


def draw_at_risk(key, part):
    key = jax.random.fold_in(key, 23)
    first, second = jax.random.split(key)
    levels = jax.random.randint(first, (1, TASKS // TB), 0, 5)
    rolls = jax.random.randint(second, (TOKENS // TB, TASKS // TB), 0, 4)
    return (rolls < levels).astype(jnp.int32)


def with_ends(array, key, smallest, largest):
    longest = array.shape.index(max(array.shape))
    spots = []
    for shift in (0, 1):
        where = [jax.random.randint(jax.random.fold_in(key, axis), (), 0, length) for axis, length in enumerate(array.shape)]
        where[longest] = (where[longest] + shift) % array.shape[longest]
        spots.append(tuple(where))
    return array.at[spots[0]].set(smallest).at[spots[1]].set(largest)


def block_levels(own_key, extent, cuts, low, high):
    def one(axis_at, parts):
        draws = jax.random.uniform(jax.random.fold_in(jax.random.fold_in(own_key, 6), axis_at), (parts,), jnp.float32, low / len(cuts), high / len(cuts))
        return jnp.repeat(jnp.exp(draws), extent[axis_at] // parts).reshape((-1,) + (1,) * (len(extent) - axis_at - 1))

    factor_of = one(*cuts[0])
    for cut in cuts[1:]:
        factor_of = factor_of * one(*cut)
    return factor_of


def scatter_about(stream_key, extent, scale, limit, cuts=(), kind=jnp.bfloat16):
    result = scale * jax.random.normal(stream_key, extent, jnp.float32)
    if cuts:
        result = result * block_levels(stream_key, extent, cuts, -0.22, 0.18)
    return jnp.clip(result, -limit, limit).astype(kind)


def setup_inputs(seed: int = 0) -> dict:
    splits = jax.random.split(jax.random.key(seed), 8)
    return {
        "features": scatter_about(splits[0], (TOKENS, BINS, E), 1.0, 6.0, ((0, 256),)),
        "task_embed": scatter_about(splits[1], (TASKS, E), E ** -0.5, 0.25, ((0, 16),)),
        "bin_bias": jnp.clip(-2.0 + 2.5 * jax.random.uniform(splits[2], (TASKS, BINS), jnp.float32) ** block_levels(splits[2], (TASKS, BINS), ((0, 16),), -0.2, 0.2), -2.0, 0.5),
        "bin_bounds": draw_bin_bounds(jax.random.fold_in(splits[7], 71), 0),
        "event_time": with_ends(jax.random.randint(splits[4], (TOKENS, TASKS), 1, 640), jax.random.fold_in(splits[4], 1), 1, 639).astype(jnp.int32),
        "censored": with_ends((jax.random.randint(splits[5], (TOKENS, TASKS), 0, 3) < 1).astype(jnp.int32), jax.random.fold_in(splits[5], 1), 0, 1),
        "at_risk": draw_at_risk(jax.random.fold_in(splits[7], 71), 0),
    }


time_unit = 0.015625


def dlogit_block(feat_wide, emb, bias, times, cens, risk, lower, spans):
    logit = jnp.einsum("tbd,kd->tbk", feat_wide, emb.astype(jnp.float32)) + bias.T[None, :, :]
    moment = times[:, None, :]
    exposure = jnp.clip(moment - lower[None, :, None], 0, spans[None, :, None]).astype(jnp.float32) * time_unit
    inside = (moment > lower[None, :, None]) & (moment <= (lower + spans)[None, :, None]) & (cens[:, None, :] == 0)
    event = inside.astype(jnp.float32)
    return risk[:, :, None].astype(jnp.float32) * (exposure * jnp.exp(logit) - event)


def reference(features, task_embed, bin_bias, bin_bounds, event_time, censored, at_risk):
    lower = bin_bounds[:-1]
    spans = bin_bounds[1:] - lower
    risk_rows = jnp.repeat(at_risk, TB, axis=0)
    feat_wide = features.astype(jnp.float32)

    def step(index, carry):
        grad_rows, grad_emb, grad_bin = carry
        start = (index * TB).astype(jnp.int32)
        emb = lax.dynamic_slice_in_dim(task_embed, start, TB, 0)
        bias = lax.dynamic_slice_in_dim(bin_bias, start, TB, 0)
        times = lax.dynamic_slice_in_dim(event_time, start, TB, 1)
        cens = lax.dynamic_slice_in_dim(censored, start, TB, 1)
        risk = lax.dynamic_slice_in_dim(risk_rows, index.astype(jnp.int32), 1, 1)
        dlogit = dlogit_block(feat_wide, emb, bias, times, cens, risk, lower, spans)
        low = dlogit.astype(jnp.bfloat16).astype(jnp.float32)
        grad_rows = grad_rows + jnp.einsum("tbk,kd->tbd", low, emb.astype(jnp.float32))
        part_emb = jnp.einsum("tbk,tbd->kd", low, feat_wide)
        grad_emb = lax.dynamic_update_slice_in_dim(grad_emb, part_emb, start, 0)
        grad_bin = lax.dynamic_update_slice_in_dim(grad_bin, jnp.sum(dlogit, axis=0).T, start, 0)
        return grad_rows, grad_emb, grad_bin

    init = (jnp.zeros((TOKENS, BINS, E), jnp.float32), jnp.zeros((TASKS, E), jnp.float32), jnp.zeros((TASKS, BINS), jnp.float32))
    grad_rows, grad_emb, grad_bin = lax.fori_loop(jnp.int32(0), jnp.int32(TASKS // TB), step, init)
    emb_scale = (TOKENS * BINS) ** -0.5
    return grad_rows.astype(jnp.bfloat16), grad_emb * emb_scale, grad_bin * (1.0 / TOKENS)
```

```python
import functools

import jax
import jax.numpy as jnp
from jax import lax
from jax.experimental import pallas as pl
from jax.experimental.pallas import tpu as pltpu
from jax.sharding import PartitionSpec as P

time_unit = 0.015625

NZ = 8
NDP = 16
BLOCK = 256


def z_shift(step):
    return [(z * 2 + h, ((z + step) % NZ) * 2 + h) for z in range(NZ) for h in range(2)]


def swap_low_bit(count):
    return [(i, i ^ 1) for i in range(count)]


def plane_groups():
    return [
        [
            ((low * 4 + x) * 2 + core) * 16 + z * 2 + h
            for h in range(2)
            for low in range(2)
            for x in range(4)
        ]
        for core in range(2)
        for z in range(NZ)
    ]


def pack_kernel(where_ref, risk_ref, time_ref, cens_ref, own_ref, other_ref):
    h = where_ref[2]
    for z in range(NZ):
        row = z // (NZ // 2)
        for side, out in ((h, own_ref), (1 - h, other_ref)):
            start = pl.multiple_of(z * 32 + side * 16, 16)
            times = time_ref[pl.ds(start, 16), :]
            signed = jnp.where(cens_ref[pl.ds(start, 16), :] == 0, times, -times)
            for k in range(4):
                cols = slice(k * 128, (k + 1) * 128)
                out[z * 16 : (z + 1) * 16, cols] = signed[:, cols] * risk_ref[row, k]


def pack_events(where, at_risk, event_time, censored):
    smem = pl.BlockSpec(memory_space=pltpu.SMEM)
    vmem = pl.BlockSpec(memory_space=pltpu.VMEM)
    half = jax.ShapeDtypeStruct((128, 512), jnp.int32)
    return pl.pallas_call(
        pack_kernel,
        out_shape=(half, half),
        in_specs=[smem, smem, vmem, vmem],
        out_specs=(vmem, vmem),
        name="pack_events",
    )(where, at_risk, event_time, censored)


SLOTS = (0, 1, -1, 2, -2, 3, -3, 4)


def main_kernel(
    where_ref,
    bounds_ref,
    f0, f1, f2, f3, f4, f5, f6, f7a, f7b,
    e0_ref, e1_ref, b0_ref, b1_ref, p0_ref, p1_ref,
    own_ref, r1, r2, r3, r4, r5, r6, r7,
    keep_ref, send_ref,
    feats, acc,
):
    step = pl.program_id(0)
    z, core, h = where_ref[0], where_ref[1], where_ref[2]

    @pl.when(step == 0)
    def _():
        for slot, ref in enumerate((f0, f1, f2, f3, f4, f5, f6)):
            feats[slot * 128 : (slot + 1) * 128, :] = ref[...]
        feats[896:960, :] = f7a[...]
        feats[960:1024, :] = f7b[...]
        acc[...] = jnp.zeros_like(acc)

    first = step < 2
    emb = jnp.where(first, e0_ref[...], e1_ref[...])
    bias = jnp.where(first, b0_ref[...], b1_ref[...])
    bins = lax.broadcasted_iota(jnp.int32, (8, BLOCK), 0)
    lower = jnp.zeros((8, BLOCK), jnp.float32)
    upper = jnp.zeros((8, BLOCK), jnp.float32)
    for b in range(8):
        lower = jnp.where(bins == b, bounds_ref[b].astype(jnp.float32) * time_unit, lower)
        upper = jnp.where(bins == b, bounds_ref[b + 1].astype(jnp.float32) * time_unit, upper)
    span = upper - lower

    g_emb = jnp.zeros((BLOCK, 512), jnp.float32)
    g_bin = jnp.zeros((8, BLOCK), jnp.float32)
    for part in range(4):
        rows = slice(part * 256, (part + 1) * 256)
        block = feats[rows, :]
        logit = lax.dot_general(
            block, emb, (((1,), (1,)), ((), ())), preferred_element_type=jnp.float32
        )
        lows = []
        for slot in (2 * part, 2 * part + 1):
            owner = lax.rem(z + (NZ - SLOTS[slot]), NZ)
            tok = pl.ds(pl.multiple_of(owner * 16, 16), 16)
            signed = jnp.where(first, p0_ref[tok, :], p1_ref[tok, :])
            signed = signed.astype(jnp.float32) * time_unit
            moment = jnp.abs(signed)
            at = (slot % 2) * 128
            piece = logit[at : at + 128].reshape(16, 8, BLOCK) + bias[None]
            exposure = jnp.clip(moment[:, None, :] - lower[None], 0.0, span[None])
            inside = (signed[:, None, :] > lower[None]) & (signed[:, None, :] <= upper[None])
            dlogit = exposure * jnp.exp(piece) - inside.astype(jnp.float32)
            g_bin = g_bin + jnp.sum(dlogit, axis=0)
            lows.append(dlogit.reshape(128, BLOCK).astype(jnp.bfloat16))
        low = jnp.concatenate(lows, axis=0)
        acc[rows, :] += jnp.dot(low, emb, preferred_element_type=jnp.float32)
        g_emb = g_emb + lax.dot_general(
            low, block, (((0,), (0,)), ((), ())), preferred_element_type=jnp.float32
        )

    h_abs = jnp.where(first, h, 1 - h)
    half = lax.rem(step, 2)
    split = g_emb.reshape(4, 2, 32, 512)
    zero, one = split[:, 0].reshape(128, 512), split[:, 1].reshape(128, 512)
    spot = pl.ds(pl.multiple_of((h_abs * 2 + half) * 128, 128), 128)
    keep_ref[spot, :] = jnp.where(core == 0, zero, one)
    send_ref[spot, :] = jnp.where(core == 0, one, zero)
    brow = pl.ds(pl.multiple_of(512 + h_abs * 8, 8), 8)
    bcol = pl.ds(pl.multiple_of(half * BLOCK, BLOCK), BLOCK)
    keep_ref[brow, bcol] = g_bin
    send_ref[brow, bcol] = g_bin

    @pl.when(step == 3)
    def _():
        own_ref[...] = acc[0:128, :]
        for slot, ref in enumerate((r1, r2, r3, r4, r5, r6, r7), 1):
            ref[...] = acc[slot * 128 : (slot + 1) * 128, :].astype(jnp.bfloat16)


def main_call(where, bounds, feats, embs, biases, events):
    def whole(rows):
        return pl.BlockSpec((rows, 512), lambda i, w, b: (0, 0))

    def early(i):
        return jnp.minimum(i, 1)

    def late(i):
        return jnp.maximum(i - 2, 0)

    in_specs = [whole(128)] * 7 + [whole(64)] * 2
    in_specs += [
        pl.BlockSpec((BLOCK, 512), lambda i, w, b: (early(i), 0)),
        pl.BlockSpec((BLOCK, 512), lambda i, w, b: (late(i), 0)),
        pl.BlockSpec((8, BLOCK), lambda i, w, b: (0, early(i))),
        pl.BlockSpec((8, BLOCK), lambda i, w, b: (0, late(i))),
        pl.BlockSpec((128, BLOCK), lambda i, w, b: (0, early(i))),
        pl.BlockSpec((128, BLOCK), lambda i, w, b: (0, late(i))),
    ]
    back = jax.ShapeDtypeStruct((128, 512), jnp.bfloat16)
    wide = jax.ShapeDtypeStruct((528, 512), jnp.float32)
    return pl.pallas_call(
        main_kernel,
        out_shape=(jax.ShapeDtypeStruct((128, 512), jnp.float32),) + (back,) * 7 + (wide, wide),
        grid_spec=pltpu.PrefetchScalarGridSpec(
            num_scalar_prefetch=2,
            grid=(4,),
            in_specs=in_specs,
            out_specs=[whole(128)] * 8 + [whole(528)] * 2,
            scratch_shapes=[
                pltpu.VMEM((1024, 512), jnp.bfloat16),
                pltpu.VMEM((1024, 512), jnp.float32),
            ],
        ),
        compiler_params=pltpu.CompilerParams(vmem_limit_bytes=40 * 1024 * 1024),
        cost_estimate=pl.CostEstimate(
            flops=3_300_000_000, bytes_accessed=8_000_000, transcendentals=1_048_576
        ),
        name="terms",
    )(where, bounds, *feats, *embs, *biases, *events)


def per_device(features, task_embed, bin_bias, bin_bounds, event_time, censored, at_risk):
    tokens_all = features.shape[0] * lax.axis_size("dp") * lax.axis_size("task")
    bins = features.shape[1]
    task, dp = lax.axis_index("task"), lax.axis_index("dp")
    z, h, core = task // 2, task % 2, dp % 2
    where = jnp.stack([z, core, h]).astype(jnp.int32)

    mine = features.reshape(128, 512)
    chunk = {0: mine}
    for step in (1, -1, 2, -2):
        chunk[step] = lax.ppermute(mine, "task", z_shift(step))
    own_p, other_p = pack_events(where, at_risk, event_time, censored)
    swap = swap_low_bit(16)
    far_p = lax.ppermute(other_p, "task", swap)
    far_emb = lax.ppermute(task_embed, "task", swap)
    bias = bin_bias.T
    far_bias = lax.ppermute(bias, "task", swap)
    chunk[3] = lax.ppermute(chunk[1], "task", z_shift(2))
    chunk[-3] = lax.ppermute(chunk[-1], "task", z_shift(-2))
    upper = lax.ppermute(chunk[2][:64], "task", z_shift(2))
    lower = lax.ppermute(chunk[-2][64:], "task", z_shift(-2))

    feats = [chunk[step] for step in SLOTS[:-1]] + [upper, lower]
    outs = main_call(
        where, bin_bounds, feats, (task_embed, far_emb), (bias, far_bias), (own_p, far_p)
    )
    own, backs, keep, send = outs[0], outs[1:8], outs[8], outs[9]

    other = lax.ppermute(send, "dp", swap)
    returned = [
        lax.ppermute(part, "task", z_shift(-step)) for part, step in zip(backs, SLOTS[1:])
    ]
    both = keep + other
    pieces = jnp.concatenate(
        [
            both[:512].reshape(2, 8, 32, 512),
            jnp.broadcast_to(both[512:].reshape(2, 1, 8, 512), (2, 8, 8, 512)),
        ],
        axis=2,
    ).astype(jnp.bfloat16)
    swapped = lax.all_to_all(
        pieces.reshape(640, 512),
        ("dp", "task"),
        0,
        0,
        tiled=True,
        axis_index_groups=plane_groups(),
    )
    total = jnp.sum(swapped.reshape(16, 40, 512).astype(jnp.float32), axis=0)
    emb_scale = (tokens_all * bins) ** (-0.5)
    grad_embed = total[:32] * emb_scale
    grad_bias = lax.dynamic_slice_in_dim(total[32:], dp * 32, 32, 1).T * (1.0 / tokens_all)

    grad = own
    for part in returned:
        grad = grad + part.astype(jnp.float32)
    return (grad.astype(jnp.bfloat16).reshape(features.shape), grad_embed, grad_bias)


def solution(mesh):
    return jax.shard_map(
        per_device,
        mesh=mesh,
        in_specs=(
            P(("dp", "task"), None, None),
            P("task", None),
            P("task", None),
            P(),
            P("dp", "task"),
            P("dp", "task"),
            P("dp", "task"),
        ),
        out_specs=(P(("dp", "task"), None, None), P(("task", "dp"), None), P(("task", "dp"), None)),
        check_vma=False,
    )
```

```python
import jax
import jax.numpy as jnp
from jax import lax
from jax.experimental import pallas as pl
from jax.experimental.pallas import tpu as pltpu
from jax.sharding import PartitionSpec as P

time_unit = 0.015625

NZ = 8
ROWS = 128
WIDE = 512
LIMIT = 40 * 1024 * 1024
BOTH = ("dp", "task")


def z_shift(step):
    return [(z * 2 + h, ((z + step) % NZ) * 2 + h) for z in range(NZ) for h in range(2)]


def z_apart(step):
    pairs = []
    for dp in range(16):
        way = step if dp % 2 == 0 else -step
        for z in range(NZ):
            for h in range(2):
                pairs.append((dp * 16 + z * 2 + h, dp * 16 + ((z + way) % NZ) * 2 + h))
    return pairs


def y_shift(step):
    pairs = []
    for y in range(4):
        there = (y + step) % 4
        for inner in range(8):
            for z in range(NZ):
                source = ((y % 2) * 8 + inner) * 16 + z * 2 + y // 2
                target = ((there % 2) * 8 + inner) * 16 + z * 2 + there // 2
                pairs.append((source, target))
    return pairs


def x_shift(step):
    return [
        ((low * 4 + x) * 2 + core, (low * 4 + (x + step) % 4) * 2 + core)
        for low in range(2)
        for x in range(4)
        for core in range(2)
    ]


def swap_low_bit():
    return [(i, i ^ 1) for i in range(16)]


def column_groups():
    return [[z * 2 + h for z in range(NZ)] for h in range(2)]


def place():
    task, dp = lax.axis_index("task"), lax.axis_index("dp")
    return task // 2, lax.rem(dp, 2), lax.rem(task, 2)


def call(kernel, name, outs, args, spaces="", to="", scratch=(), limit=LIMIT):
    kinds = {"s": pltpu.SMEM, "v": pltpu.VMEM, "a": pl.ANY, "h": pltpu.HBM}
    spaces = spaces + "v" * (len(args) - len(spaces))
    to = to + "v" * (len(outs) - len(to))
    return pl.pallas_call(
        kernel,
        out_shape=[jax.ShapeDtypeStruct(shape, kind) for shape, kind in outs],
        in_specs=[pl.BlockSpec(memory_space=kinds[space]) for space in spaces],
        out_specs=[pl.BlockSpec(memory_space=kinds[space]) for space in to],
        scratch_shapes=scratch,
        compiler_params=pltpu.CompilerParams(vmem_limit_bytes=limit),
        name=name,
    )(*args)


def pack_kernel(risk_ref, bounds_ref, time_ref, cens_ref, bias_ref, own_ref, other_ref):
    _, _, h = place()
    for z in range(NZ):
        row = z // (NZ // 2)
        for side, out in ((h, own_ref), (1 - h, other_ref)):
            start = pl.multiple_of(z * 32 + side * 16, 16)
            times = time_ref[pl.ds(start, 16), :]
            signed = jnp.where(cens_ref[pl.ds(start, 16), :] == 0, times, -times)
            for k in range(4):
                cols = slice(k * 128, (k + 1) * 128)
                live = signed[:, cols] * risk_ref[row, k]
                out[z * 16 : (z + 1) * 16, cols] = live.astype(jnp.float32) * time_unit
    own_ref[128:136, :] = bias_ref[...]
    other_ref[128:136, :] = bias_ref[...]
    bins = lax.broadcasted_iota(jnp.int32, (8, WIDE), 0)
    for k in range(2):
        edge = jnp.zeros((8, WIDE), jnp.int32)
        for b in range(8):
            edge = jnp.where(bins == b, bounds_ref[b + k], edge)
        own_ref[136 + k * 8 : 144 + k * 8, :] = edge.astype(jnp.float32) * time_unit


def grad_kernel(*refs):
    chunks, refs = refs[:8], refs[8:]
    e0, e1, p0, p1, back_ref, low_out, bin_ref, feats, embs, events, backs, low_ref, sems = refs
    z, core, _ = place()

    def fetch(source, target, slot):
        copy = pltpu.make_async_copy(source, target, sems.at[slot])
        copy.start()
        return copy

    copies = [
        fetch(chunk, feats.at[pl.ds(slot * ROWS, ROWS)], slot)
        for slot, chunk in enumerate(chunks)
    ]
    copies.append(fetch(e0, embs.at[pl.ds(0, 512)], 8))
    copies.append(fetch(p0, events.at[pl.ds(0, 152)], 9))
    copies.append(fetch(e1, embs.at[pl.ds(512, 512)], 10))
    copies.append(fetch(p1, events.at[pl.ds(152, 136)], 11))

    way = 1 - 2 * core
    shifts = (0, 1, -1, 2 * way, -2 * way, 3 * way, -3 * way, 4)
    owners = [lax.rem(z + (NZ - shift), NZ) for shift in shifts]
    for copy in copies:
        copy.wait()
    lower, upper = events[136:144, :], events[144:152, :]
    span = upper - lower

    def step(i, carry):
        out = pl.ds(pl.multiple_of(i * WIDE, WIDE), WIDE)
        emb = embs[out, :]
        base = i * 152
        bias = events[pl.ds(pl.multiple_of(base + 128, 8), 8), :]
        g_bin = jnp.zeros((8, WIDE), jnp.float32)
        for part in range(4):
            logit = lax.dot_general(
                feats[part * 256 : (part + 1) * 256, :],
                emb,
                (((1,), (1,)), ((), ())),
                preferred_element_type=jnp.float32,
            )
            for slot in (2 * part, 2 * part + 1):
                signed = events[pl.ds(pl.multiple_of(base + owners[slot] * 16, 8), 16), :]
                moment = jnp.abs(signed)[:, None, :]
                signed = signed[:, None, :]
                at = (slot % 2) * ROWS
                piece = logit[at : at + ROWS].reshape(16, 8, WIDE) + bias[None]
                exposure = jnp.clip(moment - lower[None], 0.0, span[None])
                inside = (signed > lower[None]) & (signed <= upper[None])
                dlogit = exposure * jnp.exp(piece) - inside.astype(jnp.float32)
                g_bin = g_bin + jnp.sum(dlogit, axis=0)
                low_ref[slot * ROWS : (slot + 1) * ROWS, out] = dlogit.reshape(ROWS, WIDE).astype(
                    jnp.bfloat16
                )
        bin_ref[:, out] = g_bin
        return carry

    lax.fori_loop(0, 2, step, 0)
    sent = [fetch(low_ref, low_out, 8)]
    for slot in range(0, 8, 2):
        both = jnp.dot(
            low_ref[slot * ROWS : (slot + 2) * ROWS, :],
            embs[...],
            preferred_element_type=jnp.float32,
        ).astype(jnp.bfloat16)
        backs[slot * ROWS : (slot + 2) * ROWS, :] = both
        for one in (slot, slot + 1):
            source = backs.at[pl.ds(one * ROWS, ROWS)]
            target = back_ref.at[pl.ds(pl.multiple_of(owners[one] * ROWS, ROWS), ROWS)]
            sent.append(fetch(source, target, one))
    for copy in sent:
        copy.wait()


def split_sums(sums):
    high = sums.astype(jnp.bfloat16)
    rest = (sums - high.astype(jnp.float32)).astype(jnp.bfloat16)
    return jnp.concatenate([high, rest], axis=0)


def emb_kernel(*refs):
    chunks, refs = refs[:8], refs[8:]
    low_in, bin_ref, keep_ref, send_ref, feats, low_ref, sems = refs
    copies = []
    for slot, chunk in enumerate(chunks):
        copy = pltpu.make_async_copy(
            chunk, feats.at[pl.ds(slot * ROWS, ROWS)], sems.at[slot]
        )
        copy.start()
        copies.append(copy)
    blocks = []
    for i in range(4):
        part = pl.ds(i * 256, 256)
        blocks.append(
            pltpu.make_async_copy(low_in.at[:, part], low_ref.at[:, part], sems.at[8 + i])
        )
        blocks[i].start()
    for copy in copies:
        copy.wait()
    _, core, h = place()

    for i in range(4):
        blocks[i].wait()
        g_emb = lax.dot_general(
            low_ref[:, i * 256 : (i + 1) * 256],
            feats[...],
            (((0,), (0,)), ((), ())),
            preferred_element_type=jnp.float32,
        )
        there = (h if i < 2 else 1 - h) * 2 + i % 2
        split = g_emb.reshape(4, 2, 32, 512)
        zero, one = split[:, 0].reshape(128, 512), split[:, 1].reshape(128, 512)
        spot = pl.ds(pl.multiple_of(there * 128, 128), 128)
        keep_ref[spot, :] = jnp.where(core == 0, zero, one)
        send_ref[spot, :] = jnp.where(core == 0, one, zero).astype(jnp.bfloat16)

    for side in range(2):
        sums = bin_ref[:, side * 512 : (side + 1) * 512]
        there = h if side == 0 else 1 - h
        keep_ref[pl.ds(pl.multiple_of(512 + there * 8, 8), 8), :] = sums
        send_ref[pl.ds(pl.multiple_of(512 + there * 16, 16), 16), :] = split_sums(sums)


def join_kernel(keep_ref, got_ref, own_ref, *outs):
    h, low_y = lax.rem(lax.axis_index("task"), 2), lax.axis_index("dp") // 8
    for shift in range(4):
        there = lax.rem(h * 2 + low_y + shift, 4)
        spot = pl.ds(pl.multiple_of(there * 128, 128), 128)
        rows = keep_ref[spot, :] + got_ref[spot, :].astype(jnp.float32)
        side = there // 2
        tail = got_ref[pl.ds(pl.multiple_of(512 + side * 16, 16), 16), :].astype(jnp.float32)
        sums = keep_ref[pl.ds(pl.multiple_of(512 + side * 8, 8), 8), :] + tail[0:8] + tail[8:16]
        if shift == 0:
            own_ref[0:128, :] = rows
            own_ref[128:136, :] = sums
        else:
            outs[shift - 1][0:128, :] = rows.astype(jnp.bfloat16)
            outs[shift - 1][128:144, :] = split_sums(sums)


def add_parts(own_ref, parts, rows):
    total = own_ref[0:rows, :]
    sums = own_ref[rows : rows + 8, :]
    for part in parts:
        total = total + part[0:rows, :].astype(jnp.float32)
        tail = part[rows : rows + 16, :].astype(jnp.float32)
        sums = sums + tail[0:8] + tail[8:16]
    return total, sums


def sum_y_kernel(*refs):
    own_ref, parts, mine_ref, outs, total = refs[0], refs[1:4], refs[4], refs[5:8], refs[8]
    rows, sums = add_parts(own_ref, parts, 128)
    total[...] = rows
    x = lax.rem(lax.axis_index("dp") // 2, 4)
    for shift in range(4):
        there = lax.rem(x + shift, 4)
        piece = total[pl.ds(pl.multiple_of(there * 32, 32), 32), :]
        if shift == 0:
            mine_ref[0:32, :] = piece
            mine_ref[32:40, :] = sums
        else:
            outs[shift - 1][0:32, :] = piece.astype(jnp.bfloat16)
            outs[shift - 1][32:48, :] = split_sums(sums)


def sum_x_kernel(emb_scale, bin_scale, *refs):
    own_ref, parts, emb_ref, bin_ref = refs[0], refs[1:4], refs[4], refs[5]
    rows, sums = add_parts(own_ref, parts, 32)
    emb_ref[...] = rows * emb_scale
    dp = lax.axis_index("dp")
    turned = pltpu.roll(sums, lax.rem(512 - dp * 32, 512), 1)
    bin_ref[...] = turned[:, 0:32] * bin_scale


def sum_kernel(parts_ref, out_ref):
    total = parts_ref[0:ROWS, :].astype(jnp.float32)
    for k in range(1, NZ):
        total = total + parts_ref[k * ROWS : (k + 1) * ROWS, :].astype(jnp.float32)
    out_ref[...] = total.astype(jnp.bfloat16)


def per_device(features, task_embed, bin_bias, bin_bounds, event_time, censored, at_risk):
    tokens_all = features.shape[0] * lax.axis_size("dp") * lax.axis_size("task")
    bins = features.shape[1]
    swap = swap_low_bit()
    low, wide = jnp.bfloat16, jnp.float32

    mine = features.reshape(ROWS, 512)
    far_emb = lax.ppermute(task_embed, "task", swap)
    two = lax.ppermute(mine, BOTH, z_apart(2))
    two_back = lax.ppermute(mine, BOTH, z_apart(-2))
    p0, out_p = call(
        pack_kernel,
        "pack_events",
        [((152, 512), wide), ((136, 512), wide)],
        (at_risk, bin_bounds, event_time, censored, bin_bias.T),
        "ss",
        limit=None,
    )
    p1 = lax.ppermute(out_p, "task", swap)
    three = lax.ppermute(two, BOTH, z_apart(1))
    three_back = lax.ppermute(two_back, BOTH, z_apart(-1))
    four = lax.ppermute(two, BOTH, z_apart(2))
    one = lax.ppermute(mine, "task", z_shift(1))
    one_back = lax.ppermute(mine, "task", z_shift(-1))
    chunks = (mine, one, one_back, two, two_back, three, three_back, four)

    back, lows, g_bin = call(
        grad_kernel,
        "terms",
        [((1024, 512), low), ((1024, 1024), low), ((8, 1024), wide)],
        (*chunks, task_embed, far_emb, p0, p1),
        "h" * 12,
        "hh",
        limit=None,
        scratch=[
            pltpu.VMEM((1024, 512), low),
            pltpu.VMEM((1024, 512), low),
            pltpu.VMEM((288, 512), wide),
            pltpu.VMEM((1024, 512), low),
            pltpu.VMEM((1024, 1024), low),
            pltpu.SemaphoreType.DMA((12,)),
        ],
    )
    returned = lax.all_to_all(back, "task", 0, 0, tiled=True, axis_index_groups=column_groups())

    keep, send = call(
        emb_kernel,
        "emb_terms",
        [((528, 512), wide), ((544, 512), low)],
        (*chunks, lows, g_bin),
        "h" * 9,
        limit=None,
        scratch=[
            pltpu.VMEM((1024, 512), low),
            pltpu.VMEM((1024, 1024), low),
            pltpu.SemaphoreType.DMA((12,)),
        ],
    )
    got = lax.ppermute(send, "dp", swap)
    own, *parts = call(
        join_kernel, "join_cores", [((136, 512), wide)] + [((144, 512), low)] * 3, (keep, got)
    )
    parts = [lax.ppermute(part, BOTH, y_shift(d)) for d, part in enumerate(parts, 1)]
    own, *parts = call(
        sum_y_kernel,
        "sum_y",
        [((40, 512), wide)] + [((48, 512), low)] * 3,
        (own, *parts),
        scratch=[pltpu.VMEM((128, 512), wide)],
    )
    parts = [lax.ppermute(part, "dp", x_shift(d)) for d, part in enumerate(parts, 1)]

    def sum_x(*refs):
        sum_x_kernel((tokens_all * bins) ** (-0.5), 1.0 / tokens_all, *refs)

    grad_embed, grad_bias = call(
        sum_x, "sum_x", [((32, 512), wide), ((8, 32), wide)], (own, *parts)
    )
    (grad,) = call(sum_kernel, "sum_returned", [((ROWS, 512), low)], (returned,))
    return (grad.reshape(features.shape), grad_embed, grad_bias.T)


def solution(mesh):
    return jax.shard_map(
        per_device,
        mesh=mesh,
        in_specs=(
            P(("dp", "task"), None, None),
            P("task", None),
            P("task", None),
            P(),
            P("dp", "task"),
            P("dp", "task"),
            P("dp", "task"),
        ),
        out_specs=(P(("dp", "task"), None, None), P(("task", "dp"), None), P(("task", "dp"), None)),
        check_vma=False,
    )
```

```python
import jax
import jax.numpy as jnp
from jax import lax
from jax.experimental import pallas as pl
from jax.experimental.pallas import tpu as pltpu
from jax.sharding import PartitionSpec as P

time_unit = 0.015625

NZ = 8
ROWS = 128
WIDE = 512
LIMIT = 40 * 1024 * 1024
BOTH = ("dp", "task")


def z_shift(step):
    return [(z * 2 + h, ((z + step) % NZ) * 2 + h) for z in range(NZ) for h in range(2)]


def z_apart(step):
    pairs = []
    for dp in range(16):
        way = step if dp % 2 == 0 else -step
        for z in range(NZ):
            for h in range(2):
                pairs.append((dp * 16 + z * 2 + h, dp * 16 + ((z + way) % NZ) * 2 + h))
    return pairs


def y_shift(step):
    pairs = []
    for y in range(4):
        there = (y + step) % 4
        for inner in range(8):
            for z in range(NZ):
                source = ((y % 2) * 8 + inner) * 16 + z * 2 + y // 2
                target = ((there % 2) * 8 + inner) * 16 + z * 2 + there // 2
                pairs.append((source, target))
    return pairs


def x_shift(step):
    return [
        ((low * 4 + x) * 2 + core, (low * 4 + (x + step) % 4) * 2 + core)
        for low in range(2)
        for x in range(4)
        for core in range(2)
    ]


def swap_low_bit():
    return [(i, i ^ 1) for i in range(16)]


def column_groups():
    return [[z * 2 + h for z in range(NZ)] for h in range(2)]


def place():
    task, dp = lax.axis_index("task"), lax.axis_index("dp")
    return task // 2, lax.rem(dp, 2), lax.rem(task, 2)


def call(kernel, name, outs, args, spaces="", to="", scratch=(), limit=LIMIT):
    kinds = {"s": pltpu.SMEM, "v": pltpu.VMEM, "a": pl.ANY, "h": pltpu.HBM}
    spaces = spaces + "v" * (len(args) - len(spaces))
    to = to + "v" * (len(outs) - len(to))
    return pl.pallas_call(
        kernel,
        out_shape=[jax.ShapeDtypeStruct(shape, kind) for shape, kind in outs],
        in_specs=[pl.BlockSpec(memory_space=kinds[space]) for space in spaces],
        out_specs=[pl.BlockSpec(memory_space=kinds[space]) for space in to],
        scratch_shapes=scratch,
        compiler_params=pltpu.CompilerParams(vmem_limit_bytes=limit),
        name=name,
    )(*args)


def pack_kernel(risk_ref, bounds_ref, time_ref, cens_ref, bias_ref, own_ref, other_ref):
    _, _, h = place()
    for z in range(NZ):
        row = z // (NZ // 2)
        for side, out in ((h, own_ref), (1 - h, other_ref)):
            start = pl.multiple_of(z * 32 + side * 16, 16)
            times = time_ref[pl.ds(start, 16), :]
            signed = jnp.where(cens_ref[pl.ds(start, 16), :] == 0, times, -times)
            for k in range(4):
                cols = slice(k * 128, (k + 1) * 128)
                live = signed[:, cols] * risk_ref[row, k]
                out[z * 16 : (z + 1) * 16, cols] = live.astype(jnp.float32) * time_unit
    own_ref[128:136, :] = bias_ref[...]
    other_ref[128:136, :] = bias_ref[...]
    bins = lax.broadcasted_iota(jnp.int32, (8, WIDE), 0)
    for k in range(2):
        edge = jnp.zeros((8, WIDE), jnp.int32)
        for b in range(8):
            edge = jnp.where(bins == b, bounds_ref[b + k], edge)
        own_ref[136 + k * 8 : 144 + k * 8, :] = edge.astype(jnp.float32) * time_unit


def split_sums(sums):
    high = sums.astype(jnp.bfloat16)
    rest = (sums - high.astype(jnp.float32)).astype(jnp.bfloat16)
    return jnp.concatenate([high, rest], axis=0)


def grad_kernel(*refs):
    chunks, refs = refs[:8], refs[8:]
    e0, e1, p0, p1, back_out, low_out, feat_out, bin_ref = refs[:8]
    feats, embs, events, lows, backs, sems = refs[8:]
    z, core, _ = place()

    def fetch(source, target, slot):
        copy = pltpu.make_async_copy(source, target, sems.at[slot])
        copy.start()
        return copy

    first = [
        fetch(e0, embs.at[pl.ds(0, 512)], 8),
        fetch(p0, events.at[pl.ds(0, 152)], 9),
    ]
    copies = [
        fetch(chunk, feats.at[pl.ds(slot * ROWS, ROWS)], slot)
        for slot, chunk in enumerate(chunks)
    ]
    second = [
        fetch(e1, embs.at[pl.ds(512, 512)], 10),
        fetch(p1, events.at[pl.ds(152, 136)], 11),
    ]
    way = 1 - 2 * core
    shifts = (0, 1, -1, 2 * way, -2 * way, 3 * way, -3 * way, 4)
    owners = [lax.rem(z + (NZ - shift), NZ) for shift in shifts]
    for copy in first:
        copy.wait()
    lower, upper = events[136:144, :], events[144:152, :]
    span = upper - lower

    def step(i, carry):
        out = pl.ds(i * WIDE, WIDE)
        if i == 1:
            for copy in second:
                copy.wait()

        emb = embs[out, :]
        base = i * 152
        bias = events[base + 128 : base + 136, :]
        g_bin = jnp.zeros((8, WIDE), jnp.float32)
        for part in range(4):
            if i == 0:
                copies[2 * part].wait()
                copies[2 * part + 1].wait()
            logit = lax.dot_general(
                feats[part * 256 : (part + 1) * 256, :],
                emb,
                (((1,), (1,)), ((), ())),
                preferred_element_type=jnp.float32,
            )
            for slot in (2 * part, 2 * part + 1):
                signed = events[pl.ds(pl.multiple_of(base + owners[slot] * 16, 8), 16), :]
                moment = jnp.abs(signed)[:, None, :]
                signed = signed[:, None, :]
                at = (slot % 2) * ROWS
                piece = logit[at : at + ROWS].reshape(16, 8, WIDE) + bias[None]
                exposure = jnp.clip(moment - lower[None], 0.0, span[None])
                inside = (signed > lower[None]) & (signed <= upper[None])
                dlogit = exposure * jnp.exp(piece) - inside.astype(jnp.float32)
                g_bin = g_bin + jnp.sum(dlogit, axis=0)
                lows[slot * ROWS : (slot + 1) * ROWS, out] = dlogit.reshape(ROWS, WIDE).astype(
                    jnp.bfloat16
                )
        bin_ref[:, out] = g_bin
        return carry

    stored = []
    for i in range(2):
        step(i, 0)
        if i == 0:
            stored.append(fetch(feats, feat_out, 14))
        half = pl.ds(i * WIDE, WIDE)
        stored.append(fetch(lows.at[:, half], low_out.at[:, half], 12 + i))
    sent = []
    for slot in range(0, 8, 2):
        backs[slot * ROWS : (slot + 2) * ROWS, :] = jnp.dot(
            lows[slot * ROWS : (slot + 2) * ROWS, :],
            embs[...],
            preferred_element_type=jnp.float32,
        ).astype(jnp.bfloat16)
        for one in (slot, slot + 1):
            source = backs.at[pl.ds(one * ROWS, ROWS)]
            target = back_out.at[pl.ds(pl.multiple_of(owners[one] * ROWS, ROWS), ROWS)]
            sent.append(fetch(source, target, one))
    for copy in stored + sent:
        copy.wait()


def emb_kernel(low_ref, feats, bin_ref, keep_ref, send_ref):
    _, core, h = place()
    for i in range(4):
        g_emb = lax.dot_general(
            low_ref[:, i * 256 : (i + 1) * 256],
            feats[...],
            (((0,), (0,)), ((), ())),
            preferred_element_type=jnp.float32,
        )
        there = (h if i < 2 else 1 - h) * 2 + i % 2
        split = g_emb.reshape(4, 2, 32, 512)
        zero, one = split[:, 0].reshape(128, 512), split[:, 1].reshape(128, 512)
        spot = pl.ds(pl.multiple_of(there * 128, 128), 128)
        keep_ref[spot, :] = jnp.where(core == 0, zero, one)
        send_ref[spot, :] = jnp.where(core == 0, one, zero).astype(jnp.bfloat16)
    for side in range(2):
        sums = bin_ref[:, side * 512 : (side + 1) * 512]
        there = h if side == 0 else 1 - h
        keep_ref[pl.ds(pl.multiple_of(512 + there * 8, 8), 8), :] = sums
        send_ref[pl.ds(pl.multiple_of(512 + there * 16, 16), 16), :] = split_sums(sums)


def join_kernel(keep_ref, got_ref, own_ref, *outs):
    h, low_y = lax.rem(lax.axis_index("task"), 2), lax.axis_index("dp") // 8
    for shift in range(4):
        there = lax.rem(h * 2 + low_y + shift, 4)
        spot = pl.ds(pl.multiple_of(there * 128, 128), 128)
        rows = keep_ref[spot, :] + got_ref[spot, :].astype(jnp.float32)
        side = there // 2
        tail = got_ref[pl.ds(pl.multiple_of(512 + side * 16, 16), 16), :].astype(jnp.float32)
        sums = keep_ref[pl.ds(pl.multiple_of(512 + side * 8, 8), 8), :] + tail[0:8] + tail[8:16]
        if shift == 0:
            own_ref[0:128, :] = rows
            own_ref[128:136, :] = sums
        else:
            outs[shift - 1][0:128, :] = rows.astype(jnp.bfloat16)
            outs[shift - 1][128:144, :] = split_sums(sums)


def add_parts(own_ref, parts, rows):
    total = own_ref[0:rows, :]
    sums = own_ref[rows : rows + 8, :]
    for part in parts:
        total = total + part[0:rows, :].astype(jnp.float32)
        tail = part[rows : rows + 16, :].astype(jnp.float32)
        sums = sums + tail[0:8] + tail[8:16]
    return total, sums


def sum_y_kernel(*refs):
    own_ref, parts, mine_ref, outs, total = refs[0], refs[1:4], refs[4], refs[5:8], refs[8]
    rows, sums = add_parts(own_ref, parts, 128)
    total[...] = rows
    x = lax.rem(lax.axis_index("dp") // 2, 4)
    for shift in range(4):
        there = lax.rem(x + shift, 4)
        piece = total[pl.ds(pl.multiple_of(there * 32, 32), 32), :]
        if shift == 0:
            mine_ref[0:32, :] = piece
            mine_ref[32:40, :] = sums
        else:
            outs[shift - 1][0:32, :] = piece.astype(jnp.bfloat16)
            outs[shift - 1][32:48, :] = split_sums(sums)


def sum_x_kernel(emb_scale, bin_scale, *refs):
    own_ref, parts, emb_ref, bin_ref = refs[0], refs[1:4], refs[4], refs[5]
    rows, sums = add_parts(own_ref, parts, 32)
    emb_ref[...] = rows * emb_scale
    dp = lax.axis_index("dp")
    turned = pltpu.roll(sums, lax.rem(512 - dp * 32, 512), 1)
    bin_ref[...] = turned[:, 0:32] * bin_scale


def sum_kernel(parts_ref, out_ref):
    total = parts_ref[0:ROWS, :].astype(jnp.float32)
    for k in range(1, NZ):
        total = total + parts_ref[k * ROWS : (k + 1) * ROWS, :].astype(jnp.float32)
    out_ref[...] = total.astype(jnp.bfloat16)


def per_device(features, task_embed, bin_bias, bin_bounds, event_time, censored, at_risk):
    tokens_all = features.shape[0] * lax.axis_size("dp") * lax.axis_size("task")
    bins = features.shape[1]
    swap = swap_low_bit()
    low, wide = jnp.bfloat16, jnp.float32

    mine = features.reshape(ROWS, 512)
    far_emb = lax.ppermute(task_embed, "task", swap)
    two = lax.ppermute(mine, BOTH, z_apart(2))
    two_back = lax.ppermute(mine, BOTH, z_apart(-2))
    p0, out_p = call(
        pack_kernel,
        "pack_events",
        [((152, 512), wide), ((136, 512), wide)],
        (at_risk, bin_bounds, event_time, censored, bin_bias.T),
        "ss",
        limit=None,
    )
    p1 = lax.ppermute(out_p, "task", swap)
    three = lax.ppermute(two, BOTH, z_apart(1))
    three_back = lax.ppermute(two_back, BOTH, z_apart(-1))
    four = lax.ppermute(two, BOTH, z_apart(2))
    one = lax.ppermute(mine, "task", z_shift(1))
    one_back = lax.ppermute(mine, "task", z_shift(-1))
    chunks = (mine, one, one_back, two, two_back, three, three_back, four)

    back, lows, gathered, g_bin = call(
        grad_kernel,
        "terms",
        [((1024, 512), low), ((1024, 1024), low), ((1024, 512), low), ((8, 1024), wide)],
        (*chunks, task_embed, far_emb, p0, p1),
        "h" * 12,
        "hhh",
        limit=None,
        scratch=[
            pltpu.VMEM((1024, 512), low),
            pltpu.VMEM((1024, 512), low),
            pltpu.VMEM((288, 512), wide),
            pltpu.VMEM((1024, 1024), low),
            pltpu.VMEM((1024, 512), low),
            pltpu.SemaphoreType.DMA((15,)),
        ],
    )
    returned = lax.all_to_all(back, "task", 0, 0, tiled=True, axis_index_groups=column_groups())

    keep, send = call(
        emb_kernel, "emb_terms", [((528, 512), wide), ((544, 512), low)], (lows, gathered, g_bin)
    )
    got = lax.ppermute(send, "dp", swap)
    own, *parts = call(
        join_kernel, "join_cores", [((136, 512), wide)] + [((144, 512), low)] * 3, (keep, got)
    )
    parts = [lax.ppermute(part, BOTH, y_shift(d)) for d, part in enumerate(parts, 1)]
    own, *parts = call(
        sum_y_kernel,
        "sum_y",
        [((40, 512), wide)] + [((48, 512), low)] * 3,
        (own, *parts),
        scratch=[pltpu.VMEM((128, 512), wide)],
    )
    parts = [lax.ppermute(part, "dp", x_shift(d)) for d, part in enumerate(parts, 1)]

    def sum_x(*refs):
        sum_x_kernel((tokens_all * bins) ** (-0.5), 1.0 / tokens_all, *refs)

    grad_embed, grad_bias = call(
        sum_x, "sum_x", [((32, 512), wide), ((8, 32), wide)], (own, *parts)
    )
    (grad,) = call(sum_kernel, "sum_returned", [((ROWS, 512), low)], (returned,))
    return (grad.reshape(features.shape), grad_embed, grad_bias.T)


def solution(mesh):
    return jax.shard_map(
        per_device,
        mesh=mesh,
        in_specs=(
            P(("dp", "task"), None, None),
            P("task", None),
            P("task", None),
            P(),
            P("dp", "task"),
            P("dp", "task"),
            P("dp", "task"),
        ),
        out_specs=(P(("dp", "task"), None, None), P(("task", "dp"), None), P(("task", "dp"), None)),
        check_vma=False,
    )
```

```python
import jax
import jax.numpy as jnp
from jax import lax
from jax.experimental import pallas as pl
from jax.experimental.pallas import tpu as pltpu
from jax.sharding import PartitionSpec as P

time_unit = 0.015625

NZ = 8
ROWS = 128
WIDE = 512
LIMIT = 40 * 1024 * 1024
BOTH = ("dp", "task")


def z_shift(step):
    return [(z * 2 + h, ((z + step) % NZ) * 2 + h) for z in range(NZ) for h in range(2)]


def z_apart(step):
    pairs = []
    for dp in range(16):
        way = step if dp % 2 == 0 else -step
        for z in range(NZ):
            for h in range(2):
                pairs.append((dp * 16 + z * 2 + h, dp * 16 + ((z + way) % NZ) * 2 + h))
    return pairs


def y_shift(step):
    pairs = []
    for y in range(4):
        there = (y + step) % 4
        for inner in range(8):
            for z in range(NZ):
                source = ((y % 2) * 8 + inner) * 16 + z * 2 + y // 2
                target = ((there % 2) * 8 + inner) * 16 + z * 2 + there // 2
                pairs.append((source, target))
    return pairs


def x_shift(step):
    return [
        ((low * 4 + x) * 2 + core, (low * 4 + (x + step) % 4) * 2 + core)
        for low in range(2)
        for x in range(4)
        for core in range(2)
    ]


def swap_low_bit():
    return [(i, i ^ 1) for i in range(16)]


def column_groups():
    return [[z * 2 + h for z in range(NZ)] for h in range(2)]


def place():
    task, dp = lax.axis_index("task"), lax.axis_index("dp")
    return task // 2, lax.rem(dp, 2), lax.rem(task, 2)


def call(kernel, name, outs, args, spaces="", to="", scratch=(), limit=LIMIT):
    kinds = {"s": pltpu.SMEM, "v": pltpu.VMEM, "a": pl.ANY, "h": pltpu.HBM}
    spaces = spaces + "v" * (len(args) - len(spaces))
    to = to + "v" * (len(outs) - len(to))
    return pl.pallas_call(
        kernel,
        out_shape=[jax.ShapeDtypeStruct(shape, kind) for shape, kind in outs],
        in_specs=[pl.BlockSpec(memory_space=kinds[space]) for space in spaces],
        out_specs=[pl.BlockSpec(memory_space=kinds[space]) for space in to],
        scratch_shapes=scratch,
        compiler_params=pltpu.CompilerParams(vmem_limit_bytes=limit),
        name=name,
    )(*args)


def pack_kernel(risk_ref, bounds_ref, time_ref, cens_ref, bias_ref, own_ref, other_ref):
    _, _, h = place()
    for z in range(NZ):
        row = z // (NZ // 2)
        for side, out in ((h, own_ref), (1 - h, other_ref)):
            start = pl.multiple_of(z * 32 + side * 16, 16)
            times = time_ref[pl.ds(start, 16), :]
            signed = jnp.where(cens_ref[pl.ds(start, 16), :] == 0, times, -times)
            for k in range(4):
                cols = slice(k * 128, (k + 1) * 128)
                live = signed[:, cols] * risk_ref[row, k]
                out[z * 16 : (z + 1) * 16, cols] = live.astype(jnp.float32) * time_unit
    own_ref[128:136, :] = bias_ref[...]
    other_ref[128:136, :] = bias_ref[...]
    bins = lax.broadcasted_iota(jnp.int32, (8, WIDE), 0)
    for k in range(2):
        edge = jnp.zeros((8, WIDE), jnp.int32)
        for b in range(8):
            edge = jnp.where(bins == b, bounds_ref[b + k], edge)
        own_ref[136 + k * 8 : 144 + k * 8, :] = edge.astype(jnp.float32) * time_unit


def split_sums(sums):
    high = sums.astype(jnp.bfloat16)
    rest = (sums - high.astype(jnp.float32)).astype(jnp.bfloat16)
    return jnp.concatenate([high, rest], axis=0)


def grad_kernel(*refs):
    chunks, refs = refs[:8], refs[8:]
    e0, e1, p0, p1, back_out, low_out = refs[:6]
    feats, embs, events, lows, backs, sems = refs[6:]
    z, core, _ = place()

    def fetch(source, target, slot):
        copy = pltpu.make_async_copy(source, target, sems.at[slot])
        copy.start()
        return copy

    first = [
        fetch(e0, embs.at[pl.ds(0, 512)], 8),
        fetch(p0, events.at[pl.ds(0, 152)], 9),
    ]
    copies = [
        fetch(chunk, feats.at[pl.ds(slot * ROWS, ROWS)], slot)
        for slot, chunk in enumerate(chunks)
    ]
    second = [
        fetch(e1, embs.at[pl.ds(512, 512)], 10),
        fetch(p1, events.at[pl.ds(152, 136)], 11),
    ]
    way = 1 - 2 * core
    shifts = (0, 1, -1, 2 * way, -2 * way, 3 * way, -3 * way, 4)
    owners = [lax.rem(z + (NZ - shift), NZ) for shift in shifts]
    for copy in first:
        copy.wait()
    lower, upper = events[136:144, :], events[144:152, :]
    span = upper - lower

    def step(i, carry):
        out = pl.ds(i * WIDE, WIDE)
        if i == 1:
            for copy in second:
                copy.wait()

        emb = embs[out, :]
        base = i * 152
        bias = events[base + 128 : base + 136, :]
        g_bin = jnp.zeros((8, WIDE), jnp.float32)
        for part in range(2):
            if i == 0:
                for copy in copies[4 * part : 4 * part + 4]:
                    copy.wait()
            logit = lax.dot_general(
                feats[part * 512 : (part + 1) * 512, :],
                emb,
                (((1,), (1,)), ((), ())),
                preferred_element_type=jnp.float32,
            )
            for slot in range(4 * part, 4 * part + 4):
                signed = events[pl.ds(pl.multiple_of(base + owners[slot] * 16, 8), 16), :]
                moment = jnp.abs(signed)[:, None, :]
                signed = signed[:, None, :]
                at = (slot % 4) * ROWS
                piece = logit[at : at + ROWS].reshape(16, 8, WIDE) + bias[None]
                exposure = jnp.clip(moment - lower[None], 0.0, span[None])
                inside = (signed > lower[None]) & (signed <= upper[None])
                dlogit = exposure * jnp.exp(piece) - inside.astype(jnp.float32)
                g_bin = g_bin + jnp.sum(dlogit, axis=0)
                lows[slot * ROWS : (slot + 1) * ROWS, out] = dlogit.reshape(ROWS, WIDE).astype(
                    jnp.bfloat16
                )
        lows[1024:1040, out] = split_sums(g_bin)
        return carry

    stored = []
    for i in range(2):
        step(i, 0)
        if i == 0:
            target = low_out.at[pl.ds(0, 1024), pl.ds(1024, 512)]
            stored.append(fetch(feats, target, 14))
        half = pl.ds(i * WIDE, WIDE)
        stored.append(fetch(lows.at[:, half], low_out.at[:, half], 12 + i))
    sent = []
    for slot in range(0, 8, 2):
        backs[slot * ROWS : (slot + 2) * ROWS, :] = jnp.dot(
            lows[slot * ROWS : (slot + 2) * ROWS, :],
            embs[...],
            preferred_element_type=jnp.float32,
        ).astype(jnp.bfloat16)
        for one in (slot, slot + 1):
            source = backs.at[pl.ds(one * ROWS, ROWS)]
            target = back_out.at[pl.ds(pl.multiple_of(owners[one] * ROWS, ROWS), ROWS)]
            sent.append(fetch(source, target, one))
    for copy in stored + sent:
        copy.wait()


def emb_kernel(low_ref, keep_ref, send_ref):
    _, core, h = place()
    for i in range(4):
        g_emb = lax.dot_general(
            low_ref[0:1024, i * 256 : (i + 1) * 256],
            low_ref[0:1024, 1024:1536],
            (((0,), (0,)), ((), ())),
            preferred_element_type=jnp.float32,
        )
        there = (h if i < 2 else 1 - h) * 2 + i % 2
        split = g_emb.reshape(4, 2, 32, 512)
        zero, one = split[:, 0].reshape(128, 512), split[:, 1].reshape(128, 512)
        spot = pl.ds(pl.multiple_of(there * 128, 128), 128)
        keep_ref[spot, :] = jnp.where(core == 0, zero, one)
        send_ref[spot, :] = jnp.where(core == 0, one, zero).astype(jnp.bfloat16)
    for side in range(2):
        parts = low_ref[1024:1040, side * 512 : (side + 1) * 512]
        sums = parts.astype(jnp.float32)
        there = h if side == 0 else 1 - h
        keep_ref[pl.ds(pl.multiple_of(512 + there * 8, 8), 8), :] = sums[0:8] + sums[8:16]
        send_ref[pl.ds(pl.multiple_of(512 + there * 16, 16), 16), :] = parts


def join_kernel(keep_ref, got_ref, own_ref, *outs):
    h, low_y = lax.rem(lax.axis_index("task"), 2), lax.axis_index("dp") // 8
    for shift in range(4):
        there = lax.rem(h * 2 + low_y + shift, 4)
        spot = pl.ds(pl.multiple_of(there * 128, 128), 128)
        rows = keep_ref[spot, :] + got_ref[spot, :].astype(jnp.float32)
        side = there // 2
        tail = got_ref[pl.ds(pl.multiple_of(512 + side * 16, 16), 16), :].astype(jnp.float32)
        sums = keep_ref[pl.ds(pl.multiple_of(512 + side * 8, 8), 8), :] + tail[0:8] + tail[8:16]
        if shift == 0:
            own_ref[0:128, :] = rows
            own_ref[128:136, :] = sums
        else:
            outs[shift - 1][0:128, :] = rows.astype(jnp.bfloat16)
            outs[shift - 1][128:144, :] = split_sums(sums)


def add_parts(own_ref, parts, rows):
    total = own_ref[0:rows, :]
    sums = own_ref[rows : rows + 8, :]
    for part in parts:
        total = total + part[0:rows, :].astype(jnp.float32)
        tail = part[rows : rows + 16, :].astype(jnp.float32)
        sums = sums + tail[0:8] + tail[8:16]
    return total, sums


def sum_y_kernel(*refs):
    own_ref, parts, mine_ref, outs, total = refs[0], refs[1:4], refs[4], refs[5:8], refs[8]
    rows, sums = add_parts(own_ref, parts, 128)
    total[...] = rows
    x = lax.rem(lax.axis_index("dp") // 2, 4)
    for shift in range(4):
        there = lax.rem(x + shift, 4)
        piece = total[pl.ds(pl.multiple_of(there * 32, 32), 32), :]
        if shift == 0:
            mine_ref[0:32, :] = piece
            mine_ref[32:40, :] = sums
        else:
            outs[shift - 1][0:32, :] = piece.astype(jnp.bfloat16)
            outs[shift - 1][32:48, :] = split_sums(sums)


def sum_x_kernel(emb_scale, bin_scale, *refs):
    own_ref, parts, emb_ref, bin_ref = refs[0], refs[1:4], refs[4], refs[5]
    rows, sums = add_parts(own_ref, parts, 32)
    emb_ref[...] = rows * emb_scale
    dp = lax.axis_index("dp")
    turned = pltpu.roll(sums, lax.rem(512 - dp * 32, 512), 1)
    bin_ref[...] = turned[:, 0:32] * bin_scale


def sum_kernel(parts_ref, out_ref):
    total = parts_ref[0:ROWS, :].astype(jnp.float32)
    for k in range(1, NZ):
        total = total + parts_ref[k * ROWS : (k + 1) * ROWS, :].astype(jnp.float32)
    out_ref[...] = total.astype(jnp.bfloat16)


def per_device(features, task_embed, bin_bias, bin_bounds, event_time, censored, at_risk):
    tokens_all = features.shape[0] * lax.axis_size("dp") * lax.axis_size("task")
    bins = features.shape[1]
    swap = swap_low_bit()
    low, wide = jnp.bfloat16, jnp.float32

    mine = features.reshape(ROWS, 512)
    far_emb = lax.ppermute(task_embed, "task", swap)
    two = lax.ppermute(mine, BOTH, z_apart(2))
    two_back = lax.ppermute(mine, BOTH, z_apart(-2))
    p0, out_p = call(
        pack_kernel,
        "pack_events",
        [((152, 512), wide), ((136, 512), wide)],
        (at_risk, bin_bounds, event_time, censored, bin_bias.T),
        "ss",
        limit=None,
    )
    p1 = lax.ppermute(out_p, "task", swap)
    three = lax.ppermute(two, BOTH, z_apart(1))
    three_back = lax.ppermute(two_back, BOTH, z_apart(-1))
    four = lax.ppermute(two, BOTH, z_apart(2))
    one = lax.ppermute(mine, "task", z_shift(1))
    one_back = lax.ppermute(mine, "task", z_shift(-1))
    chunks = (mine, one, one_back, two, two_back, three, three_back, four)

    back, lows = call(
        grad_kernel,
        "terms",
        [((1024, 512), low), ((1040, 1536), low)],
        (*chunks, task_embed, far_emb, p0, p1),
        "h" * 12,
        "hh",
        limit=None,
        scratch=[
            pltpu.VMEM((1024, 512), low),
            pltpu.VMEM((1024, 512), low),
            pltpu.VMEM((288, 512), wide),
            pltpu.VMEM((1040, 1024), low),
            pltpu.VMEM((1024, 512), low),
            pltpu.SemaphoreType.DMA((15,)),
        ],
    )
    returned = lax.all_to_all(back, "task", 0, 0, tiled=True, axis_index_groups=column_groups())

    keep, send = call(
        emb_kernel, "emb_terms", [((528, 512), wide), ((544, 512), low)], (lows,)
    )
    got = lax.ppermute(send, "dp", swap)
    own, *parts = call(
        join_kernel, "join_cores", [((136, 512), wide)] + [((144, 512), low)] * 3, (keep, got)
    )
    parts = [lax.ppermute(part, BOTH, y_shift(d)) for d, part in enumerate(parts, 1)]
    own, *parts = call(
        sum_y_kernel,
        "sum_y",
        [((40, 512), wide)] + [((48, 512), low)] * 3,
        (own, *parts),
        scratch=[pltpu.VMEM((128, 512), wide)],
    )
    parts = [lax.ppermute(part, "dp", x_shift(d)) for d, part in enumerate(parts, 1)]

    def sum_x(*refs):
        sum_x_kernel((tokens_all * bins) ** (-0.5), 1.0 / tokens_all, *refs)

    grad_embed, grad_bias = call(
        sum_x, "sum_x", [((32, 512), wide), ((8, 32), wide)], (own, *parts)
    )
    (grad,) = call(sum_kernel, "sum_returned", [((ROWS, 512), low)], (returned,))
    return (grad.reshape(features.shape), grad_embed, grad_bias.T)


def solution(mesh):
    return jax.shard_map(
        per_device,
        mesh=mesh,
        in_specs=(
            P(("dp", "task"), None, None),
            P("task", None),
            P("task", None),
            P(),
            P("dp", "task"),
            P("dp", "task"),
            P("dp", "task"),
        ),
        out_specs=(P(("dp", "task"), None, None), P(("task", "dp"), None), P(("task", "dp"), None)),
        check_vma=False,
    )
```

```python
import jax
import jax.numpy as jnp
from jax import lax
from jax.experimental import pallas as pl
from jax.experimental.pallas import tpu as pltpu
from jax.sharding import PartitionSpec as P

time_unit = 0.015625

NZ = 8
ROWS = 128
WIDE = 512
LIMIT = 40 * 1024 * 1024
BOTH = ("dp", "task")


def z_shift(step):
    return [(z * 2 + h, ((z + step) % NZ) * 2 + h) for z in range(NZ) for h in range(2)]


def z_apart(step):
    pairs = []
    for dp in range(16):
        way = step if dp % 2 == 0 else -step
        for z in range(NZ):
            for h in range(2):
                pairs.append((dp * 16 + z * 2 + h, dp * 16 + ((z + way) % NZ) * 2 + h))
    return pairs


def y_shift(step):
    pairs = []
    for y in range(4):
        there = (y + step) % 4
        for inner in range(8):
            for z in range(NZ):
                source = ((y % 2) * 8 + inner) * 16 + z * 2 + y // 2
                target = ((there % 2) * 8 + inner) * 16 + z * 2 + there // 2
                pairs.append((source, target))
    return pairs


def x_shift(step):
    return [
        ((low * 4 + x) * 2 + core, (low * 4 + (x + step) % 4) * 2 + core)
        for low in range(2)
        for x in range(4)
        for core in range(2)
    ]


def swap_low_bit():
    return [(i, i ^ 1) for i in range(16)]


def column_groups():
    return [[z * 2 + h for z in range(NZ)] for h in range(2)]


def place():
    task, dp = lax.axis_index("task"), lax.axis_index("dp")
    return task // 2, lax.rem(dp, 2), lax.rem(task, 2)


def call(kernel, name, outs, args, spaces="", to="", scratch=(), limit=LIMIT):
    kinds = {"s": pltpu.SMEM, "v": pltpu.VMEM, "a": pl.ANY, "h": pltpu.HBM}
    spaces = spaces + "v" * (len(args) - len(spaces))
    to = to + "v" * (len(outs) - len(to))
    return pl.pallas_call(
        kernel,
        out_shape=[jax.ShapeDtypeStruct(shape, kind) for shape, kind in outs],
        in_specs=[pl.BlockSpec(memory_space=kinds[space]) for space in spaces],
        out_specs=[pl.BlockSpec(memory_space=kinds[space]) for space in to],
        scratch_shapes=scratch,
        compiler_params=pltpu.CompilerParams(vmem_limit_bytes=limit),
        name=name,
    )(*args)


def pack_kernel(risk_ref, bounds_ref, time_ref, cens_ref, bias_ref, own_ref, other_ref):
    _, _, h = place()
    for z in range(NZ):
        row = z // (NZ // 2)
        for side, out in ((h, own_ref), (1 - h, other_ref)):
            start = pl.multiple_of(z * 32 + side * 16, 16)
            times = time_ref[pl.ds(start, 16), :]
            signed = jnp.where(cens_ref[pl.ds(start, 16), :] == 0, times, -times)
            for k in range(4):
                cols = slice(k * 128, (k + 1) * 128)
                live = signed[:, cols] * risk_ref[row, k]
                out[z * 16 : (z + 1) * 16, cols] = live.astype(jnp.float32) * time_unit
    own_ref[128:136, :] = bias_ref[...]
    other_ref[128:136, :] = bias_ref[...]
    bins = lax.broadcasted_iota(jnp.int32, (8, WIDE), 0)
    for k in range(2):
        edge = jnp.zeros((8, WIDE), jnp.int32)
        for b in range(8):
            edge = jnp.where(bins == b, bounds_ref[b + k], edge)
        own_ref[136 + k * 8 : 144 + k * 8, :] = edge.astype(jnp.float32) * time_unit


def split_sums(sums):
    high = sums.astype(jnp.bfloat16)
    rest = (sums - high.astype(jnp.float32)).astype(jnp.bfloat16)
    return jnp.concatenate([high, rest], axis=0)


def grad_kernel(*refs):
    chunks, refs = refs[:8], refs[8:]
    e0, e1, p0, p1, back_out, low_out = refs[:6]
    feats, embs, events, lows, backs, sems = refs[6:]
    z, core, _ = place()

    def fetch(source, target, slot):
        copy = pltpu.make_async_copy(source, target, sems.at[slot])
        copy.start()
        return copy

    first = [
        fetch(e0, embs.at[pl.ds(0, 512)], 8),
        fetch(p0, events.at[pl.ds(0, 152)], 9),
    ]
    copies = [
        fetch(chunk, feats.at[pl.ds(slot * ROWS, ROWS)], slot)
        for slot, chunk in enumerate(chunks)
    ]
    second = [
        fetch(e1, embs.at[pl.ds(512, 512)], 10),
        fetch(p1, events.at[pl.ds(152, 136)], 11),
    ]
    way = 1 - 2 * core
    shifts = (0, 1, -1, 2 * way, -2 * way, 3 * way, -3 * way, 4)
    owners = [lax.rem(z + (NZ - shift), NZ) for shift in shifts]
    for copy in first:
        copy.wait()
    lower, upper = events[136:144, :], events[144:152, :]
    span = upper - lower

    def step(i, carry):
        out = pl.ds(i * WIDE, WIDE)
        if i == 1:
            for copy in second:
                copy.wait()

        emb = embs[out, :]
        base = i * 152
        bias = events[base + 128 : base + 136, :]
        g_bin = jnp.zeros((8, WIDE), jnp.float32)
        for part in range(2):
            if i == 0:
                for copy in copies[4 * part : 4 * part + 4]:
                    copy.wait()
            logit = lax.dot_general(
                feats[part * 512 : (part + 1) * 512, :],
                emb,
                (((1,), (1,)), ((), ())),
                preferred_element_type=jnp.float32,
            )
            for slot in range(4 * part, 4 * part + 4):
                signed = events[pl.ds(pl.multiple_of(base + owners[slot] * 16, 8), 16), :]
                moment = jnp.abs(signed)[:, None, :]
                signed = signed[:, None, :]
                at = (slot % 4) * ROWS
                piece = logit[at : at + ROWS].reshape(16, 8, WIDE) + bias[None]
                exposure = jnp.clip(moment - lower[None], 0.0, span[None])
                inside = (signed > lower[None]) & (signed <= upper[None])
                dlogit = exposure * jnp.exp(piece) - inside.astype(jnp.float32)
                g_bin = g_bin + jnp.sum(dlogit, axis=0)
                lows[slot * ROWS : (slot + 1) * ROWS, out] = dlogit.reshape(ROWS, WIDE).astype(
                    jnp.bfloat16
                )
        lows[1024:1040, out] = split_sums(g_bin)
        return carry

    stored = []
    for i in range(2):
        step(i, 0)
        if i == 0:
            target = low_out.at[pl.ds(0, 1024), pl.ds(1024, 512)]
            stored.append(fetch(feats, target, 14))
        half = pl.ds(i * WIDE, WIDE)
        stored.append(fetch(lows.at[:, half], low_out.at[:, half], 12 + i))
    sent = []
    for slot in range(0, 8, 4):
        rows = slice(slot * ROWS, (slot + 4) * ROWS)
        backs[rows, :] = jnp.dot(
            lows[rows, :], embs[...], preferred_element_type=jnp.float32
        ).astype(jnp.bfloat16)
        for one in range(slot, slot + 4):
            source = backs.at[pl.ds(one * ROWS, ROWS)]
            target = back_out.at[pl.ds(pl.multiple_of(owners[one] * ROWS, ROWS), ROWS)]
            sent.append(fetch(source, target, one))
    for copy in stored + sent:
        copy.wait()


def emb_kernel(low_ref, keep_ref, send_ref):
    _, core, h = place()
    for i in range(4):
        g_emb = lax.dot_general(
            low_ref[0:1024, i * 256 : (i + 1) * 256],
            low_ref[0:1024, 1024:1536],
            (((0,), (0,)), ((), ())),
            preferred_element_type=jnp.float32,
        )
        there = (h if i < 2 else 1 - h) * 2 + i % 2
        split = g_emb.reshape(4, 2, 32, 512)
        zero, one = split[:, 0].reshape(128, 512), split[:, 1].reshape(128, 512)
        spot = pl.ds(pl.multiple_of(there * 128, 128), 128)
        keep_ref[spot, :] = jnp.where(core == 0, zero, one)
        send_ref[spot, :] = jnp.where(core == 0, one, zero).astype(jnp.bfloat16)
    for side in range(2):
        parts = low_ref[1024:1040, side * 512 : (side + 1) * 512]
        sums = parts.astype(jnp.float32)
        there = h if side == 0 else 1 - h
        keep_ref[pl.ds(pl.multiple_of(512 + there * 8, 8), 8), :] = sums[0:8] + sums[8:16]
        send_ref[pl.ds(pl.multiple_of(512 + there * 16, 16), 16), :] = parts


def join_kernel(keep_ref, got_ref, own_ref, *outs):
    h, low_y = lax.rem(lax.axis_index("task"), 2), lax.axis_index("dp") // 8
    for shift in range(4):
        there = lax.rem(h * 2 + low_y + shift, 4)
        spot = pl.ds(pl.multiple_of(there * 128, 128), 128)
        rows = keep_ref[spot, :] + got_ref[spot, :].astype(jnp.float32)
        side = there // 2
        tail = got_ref[pl.ds(pl.multiple_of(512 + side * 16, 16), 16), :].astype(jnp.float32)
        sums = keep_ref[pl.ds(pl.multiple_of(512 + side * 8, 8), 8), :] + tail[0:8] + tail[8:16]
        if shift == 0:
            own_ref[0:128, :] = rows
            own_ref[128:136, :] = sums
        else:
            outs[shift - 1][0:128, :] = rows.astype(jnp.bfloat16)
            outs[shift - 1][128:144, :] = split_sums(sums)


def add_parts(own_ref, parts, rows):
    total = own_ref[0:rows, :]
    sums = own_ref[rows : rows + 8, :]
    for part in parts:
        total = total + part[0:rows, :].astype(jnp.float32)
        tail = part[rows : rows + 16, :].astype(jnp.float32)
        sums = sums + tail[0:8] + tail[8:16]
    return total, sums


def sum_y_kernel(*refs):
    own_ref, parts, mine_ref, outs, total = refs[0], refs[1:4], refs[4], refs[5:8], refs[8]
    rows, sums = add_parts(own_ref, parts, 128)
    total[...] = rows
    x = lax.rem(lax.axis_index("dp") // 2, 4)
    for shift in range(4):
        there = lax.rem(x + shift, 4)
        piece = total[pl.ds(pl.multiple_of(there * 32, 32), 32), :]
        if shift == 0:
            mine_ref[0:32, :] = piece
            mine_ref[32:40, :] = sums
        else:
            outs[shift - 1][0:32, :] = piece.astype(jnp.bfloat16)
            outs[shift - 1][32:48, :] = split_sums(sums)


def sum_x_kernel(emb_scale, bin_scale, *refs):
    own_ref, parts, emb_ref, bin_ref = refs[0], refs[1:4], refs[4], refs[5]
    rows, sums = add_parts(own_ref, parts, 32)
    emb_ref[...] = rows * emb_scale
    dp = lax.axis_index("dp")
    turned = pltpu.roll(sums, lax.rem(512 - dp * 32, 512), 1)
    bin_ref[...] = turned[:, 0:32] * bin_scale


def sum_kernel(parts_ref, out_ref):
    total = parts_ref[0:ROWS, :].astype(jnp.float32)
    for k in range(1, NZ):
        total = total + parts_ref[k * ROWS : (k + 1) * ROWS, :].astype(jnp.float32)
    out_ref[...] = total.astype(jnp.bfloat16)


def per_device(features, task_embed, bin_bias, bin_bounds, event_time, censored, at_risk):
    tokens_all = features.shape[0] * lax.axis_size("dp") * lax.axis_size("task")
    bins = features.shape[1]
    swap = swap_low_bit()
    low, wide = jnp.bfloat16, jnp.float32

    mine = features.reshape(ROWS, 512)
    far_emb = lax.ppermute(task_embed, "task", swap)
    two = lax.ppermute(mine, BOTH, z_apart(2))
    two_back = lax.ppermute(mine, BOTH, z_apart(-2))
    p0, out_p = call(
        pack_kernel,
        "pack_events",
        [((152, 512), wide), ((136, 512), wide)],
        (at_risk, bin_bounds, event_time, censored, bin_bias.T),
        "ss",
        limit=None,
    )
    p1 = lax.ppermute(out_p, "task", swap)
    three = lax.ppermute(two, BOTH, z_apart(1))
    three_back = lax.ppermute(two_back, BOTH, z_apart(-1))
    four = lax.ppermute(two, BOTH, z_apart(2))
    one = lax.ppermute(mine, "task", z_shift(1))
    one_back = lax.ppermute(mine, "task", z_shift(-1))
    chunks = (mine, one, one_back, two, two_back, three, three_back, four)

    back, lows = call(
        grad_kernel,
        "terms",
        [((1024, 512), low), ((1040, 1536), low)],
        (*chunks, task_embed, far_emb, p0, p1),
        "h" * 12,
        "hh",
        limit=None,
        scratch=[
            pltpu.VMEM((1024, 512), low),
            pltpu.VMEM((1024, 512), low),
            pltpu.VMEM((288, 512), wide),
            pltpu.VMEM((1040, 1024), low),
            pltpu.VMEM((1024, 512), low),
            pltpu.SemaphoreType.DMA((15,)),
        ],
    )
    returned = lax.all_to_all(back, "task", 0, 0, tiled=True, axis_index_groups=column_groups())

    keep, send = call(
        emb_kernel, "emb_terms", [((528, 512), wide), ((544, 512), low)], (lows,)
    )
    got = lax.ppermute(send, "dp", swap)
    own, *parts = call(
        join_kernel, "join_cores", [((136, 512), wide)] + [((144, 512), low)] * 3, (keep, got)
    )
    parts = [lax.ppermute(part, BOTH, y_shift(d)) for d, part in enumerate(parts, 1)]
    own, *parts = call(
        sum_y_kernel,
        "sum_y",
        [((40, 512), wide)] + [((48, 512), low)] * 3,
        (own, *parts),
        scratch=[pltpu.VMEM((128, 512), wide)],
    )
    parts = [lax.ppermute(part, "dp", x_shift(d)) for d, part in enumerate(parts, 1)]

    def sum_x(*refs):
        sum_x_kernel((tokens_all * bins) ** (-0.5), 1.0 / tokens_all, *refs)

    grad_embed, grad_bias = call(
        sum_x, "sum_x", [((32, 512), wide), ((8, 32), wide)], (own, *parts)
    )
    (grad,) = call(sum_kernel, "sum_returned", [((ROWS, 512), low)], (returned,))
    return (grad.reshape(features.shape), grad_embed, grad_bias.T)


def solution(mesh):
    return jax.shard_map(
        per_device,
        mesh=mesh,
        in_specs=(
            P(("dp", "task"), None, None),
            P("task", None),
            P("task", None),
            P(),
            P("dp", "task"),
            P("dp", "task"),
            P("dp", "task"),
        ),
        out_specs=(P(("dp", "task"), None, None), P(("task", "dp"), None), P(("task", "dp"), None)),
        check_vma=False,
    )
```
